32 devices in a mesh: dom: 2 (over x), tensor: 16 (over z, y, core).
Axes of the slice: x: 2, y: 2, z: 4, core: 2. Of those that a mesh axis runs over, the one named last changes fastest.
Arguments:
- attn_input: bfloat16 [8, 512, 8192], P('dom', None, 'tensor'), parts along dimension 0, may hold values from -6 to 6
- grad_query: bfloat16 [8, 512, 8192], P('dom', None, 'tensor'), parts along dimension 0, may hold values from -24 to 24
- grad_key_value: bfloat16 [8, 512, 2, 1024], P('dom', None, None, 'tensor'), parts along dimension 0, may hold values from -24 to 24
- attn_mixed: bfloat16 [8, 512, 8192], P('dom', None, 'tensor'), parts along dimension 0, may hold values from -6 to 6
- grad_attn_out: bfloat16 [8, 512, 8192], P('dom', None, 'tensor'), parts along dimension 0, may hold values from -24 to 24
- mlp_input: bfloat16 [8, 512, 8192], P('dom', None, 'tensor'), parts along dimension 0, may hold values from -6 to 6
- grad_gate_up: bfloat16 [8, 512, 2, 28672], P('dom', None, None, 'tensor'), parts along dimension 0, may hold values from -24 to 24
- hidden_acts: bfloat16 [8, 512, 28672], P('dom', None, 'tensor'), parts along dimension 0, may hold values from -6 to 6
- grad_mlp_out: bfloat16 [8, 512, 8192], P('dom', None, 'tensor'), parts along dimension 0, may hold values from -24 to 24
- in_attn: bfloat16 [3, 8192, 64], P(None, 'tensor'), may hold values from -0.0625 to 0.0625
- in_mixed: bfloat16 [8192, 64], P('tensor'), may hold values from -0.0625 to 0.0625
- in_mlp: bfloat16 [2, 8192, 64], P(None, 'tensor'), may hold values from -0.0625 to 0.0625
- in_hidden: bfloat16 [28672, 64], P('tensor'), may hold values from -0.03125 to 0.03125
- out_query: bfloat16 [8192, 64], P('tensor'), may hold values from -0.0625 to 0.0625
- out_key_value: bfloat16 [2, 1024, 64], P(None, 'tensor'), may hold values from -0.1875 to 0.1875
- out_attn: bfloat16 [8192, 64], P('tensor'), may hold values from -0.0625 to 0.0625
- out_gate_up: bfloat16 [2, 28672, 64], P(None, 'tensor'), may hold values from -0.03125 to 0.03125
- out_mlp: bfloat16 [8192, 64], P('tensor'), may hold values from -0.0625 to 0.0625
- queries: bfloat16 [256, 28672], P(None, 'tensor'), may hold values from -0.125 to 0.125
- lengths: int32 [8], P('dom'), parts along dimension 0, may hold values from 1 to 512, 1024 in all
Outputs:
- train_grads: bfloat16 [8, 28672], P('dom', 'tensor'), parts along dimension 0
- scores: float32 [8, 256], P('dom', 'tensor'), parts along dimension 0
The draws below stay inside these ranges and needn't reach their ends.
There are 2 independent parts, one for each index of `dom`. The reference program is written for one: setup_inputs(seed, part) draws one part's arguments, and reference() takes and returns one part's arrays. A program takes and returns all parts, laid end to end along the dimension named above; an argument that names none is the same for every part. Nothing has to cross between parts.
Inputs may be any that keep to these rules, and one draw needn't show every extreme that they name: The lengths of one job sum to 1024, and the largest is 512.
All inputs are finite; a program needn't handle non-finite values.
Results may differ from the reference program's by a relative error of at most 0.0032.
Values sent between devices are 32-bit elements; how exact they have to be, the bound alone decides.
A program may use at most 192 MiB of HBM per device.

```python
import math
import jax
import jax.numpy as jnp
import numpy as np
from jax import lax

D = 8192
KV = 1024
FF = 28672
R = 64
SEQS = 4
MAXLEN = 512
QUERIES = 256
LIVE = 1024


def block_scale(own_key, shape, pieces, least, top_value):
    loudness, own = 1.0, jax.random.fold_in(own_key, 6)
    for position, blocks in pieces:
        steps = jnp.exp(jax.random.uniform(jax.random.fold_in(own, position), (blocks,), jnp.float32, least / len(pieces), top_value / len(pieces)))
        loudness = loudness * jnp.repeat(steps, shape[position] // blocks).reshape([-1 if axis == position else 1 for axis in range(len(shape))])
    return loudness


def length_profile(number_of, total, bound, lean):
    portions = [(1 << 20) // math.isqrt(standing ** lean) + 1 for standing in range(2, number_of + 1)]
    surplus, holding = total - bound - (number_of - 1), [1] * (number_of - 1)
    while surplus > 0:
        candidates = [i for i in range(number_of - 1) if holding[i] < bound]
        whole, budget = sum([portions[i] for i in candidates]), surplus
        for i in candidates:
            more = min(bound - holding[i], max(1, budget * portions[i] // whole), surplus)
            holding[i] = holding[i] + more
            surplus = surplus - more
    return np.array([bound] + holding)


def ragged_sizes(stream_key, count, total, limit, skew):
    if count == 2:
        one = jax.random.randint(stream_key, (), max(1, total - limit), min(limit, total - 1) + 1)
        return jnp.stack([one, total - one])
    sizes = jnp.asarray(length_profile(count, total, limit, skew), jnp.int32)
    twos = (count - 1) // 2
    giver, sink = sizes[1:1 + 2 * twos:2], sizes[2:2 + 2 * twos:2]
    slack = jnp.minimum(giver - 1, limit - sink)
    shifted = jax.random.randint(jax.random.fold_in(stream_key, 1), (twos,), 0, 1 << 20) % (slack + 1)
    sizes = sizes.at[1:1 + 2 * twos:2].set(giver - shifted).at[2:2 + 2 * twos:2].set(sink + shifted)
    return sizes[jax.random.permutation(jax.random.fold_in(stream_key, 2), count)]


def normal_values(stream_key, extent, spread, bound, cuts=(), held_as=jnp.bfloat16):
    level = block_scale(stream_key, extent, cuts, -0.22, 0.18) if cuts else 1.0
    result = jax.random.normal(stream_key, extent, jnp.float32) * spread * level
    return jnp.minimum(jnp.maximum(result, -bound), bound).astype(held_as)


def setup_inputs(seed: int = 0, part: int = 0) -> dict:
    seeds = jax.random.split(jax.random.key(seed), 21)
    own_keys = jax.random.split(jax.random.fold_in(seeds[20], part), 21)
    attn_input = normal_values(own_keys[0], (SEQS, MAXLEN, D), 1.0, 6.0, ((2, 16),))
    grad_query = normal_values(own_keys[1], (SEQS, MAXLEN, D), 4.0, 24.0, ((2, 16),))
    grad_key_value = normal_values(own_keys[2], (SEQS, MAXLEN, 2, KV), 4.0, 24.0, ((3, 16),))
    attn_mixed = normal_values(own_keys[3], (SEQS, MAXLEN, D), 1.0, 6.0, ((2, 16),))
    grad_attn_out = normal_values(own_keys[4], (SEQS, MAXLEN, D), 4.0, 24.0, ((2, 16),))
    mlp_input = normal_values(own_keys[5], (SEQS, MAXLEN, D), 1.0, 6.0, ((2, 16),))
    grad_gate_up = normal_values(own_keys[6], (SEQS, MAXLEN, 2, FF), 4.0, 24.0, ((3, 16),))
    hidden_acts = normal_values(own_keys[7], (SEQS, MAXLEN, FF), 1.0, 6.0, ((2, 16),))
    grad_mlp_out = normal_values(own_keys[8], (SEQS, MAXLEN, D), 4.0, 24.0, ((2, 16),))
    in_attn = normal_values(seeds[9], (3, D, R), D ** -0.5, 0.0625, ((1, 16),))
    in_mixed = normal_values(seeds[10], (D, R), D ** -0.5, 0.0625, ((0, 16),))
    in_mlp = normal_values(seeds[11], (2, D, R), D ** -0.5, 0.0625, ((1, 16),))
    in_hidden = normal_values(seeds[12], (FF, R), FF ** -0.5, 0.03125, ((0, 16),))
    out_query = normal_values(seeds[13], (D, R), D ** -0.5, 0.0625, ((0, 16),))
    out_key_value = normal_values(seeds[14], (2, KV, R), KV ** -0.5, 0.1875, ((1, 16),))
    out_attn = normal_values(seeds[15], (D, R), D ** -0.5, 0.0625, ((0, 16),))
    out_gate_up = normal_values(seeds[16], (2, FF, R), FF ** -0.5, 0.03125, ((1, 16),))
    out_mlp = normal_values(seeds[17], (D, R), D ** -0.5, 0.0625, ((0, 16),))
    queries = normal_values(seeds[18], (QUERIES, 7 * R * R), 0.02, 0.125, ((1, 16),))
    lengths = ragged_sizes(own_keys[19], SEQS, LIVE, MAXLEN, 2).astype(jnp.int32)
    return {"attn_input": attn_input, "grad_query": grad_query, "grad_key_value": grad_key_value, "attn_mixed": attn_mixed, "grad_attn_out": grad_attn_out, "mlp_input": mlp_input, "grad_gate_up": grad_gate_up, "hidden_acts": hidden_acts, "grad_mlp_out": grad_mlp_out, "in_attn": in_attn, "in_mixed": in_mixed, "in_mlp": in_mlp, "in_hidden": in_hidden, "out_query": out_query, "out_key_value": out_key_value, "out_attn": out_attn, "out_gate_up": out_gate_up, "out_mlp": out_mlp, "queries": queries, "lengths": lengths}


def module_grads(inputs, factor_in, gradients, factor_out, weight):
    row_total = weight.shape[0]
    in_proj = jnp.dot(inputs.reshape(row_total, -1), factor_in, preferred_element_type=jnp.float32)
    out_proj = jnp.dot(gradients.reshape(row_total, -1), factor_out, preferred_element_type=jnp.float32)
    return jnp.einsum("rs,ri,rj->sij", weight, in_proj, out_proj, precision=lax.Precision.HIGHEST)


def reference(attn_input, grad_query, grad_key_value, attn_mixed, grad_attn_out, mlp_input, grad_gate_up, hidden_acts, grad_mlp_out, in_attn, in_mixed, in_mlp, in_hidden, out_query, out_key_value, out_attn, out_gate_up, out_mlp, queries, lengths):
    row_ids = jnp.arange(SEQS * MAXLEN, dtype=jnp.int32)
    owner_seq = row_ids // MAXLEN
    offset = row_ids - owner_seq * MAXLEN
    matches = owner_seq[:, None] == jnp.arange(SEQS, dtype=jnp.int32)[None, :]
    seq_len = jnp.sum(jnp.where(matches, lengths[None, :], 0), axis=1)
    weight = (matches & (offset < seq_len)[:, None]).astype(jnp.float32) / lengths.astype(jnp.float32)[None, :]
    blocks = [
        module_grads(attn_input, in_attn[0], grad_query, out_query, weight),
        module_grads(attn_input, in_attn[1], grad_key_value[:, :, 0], out_key_value[0], weight),
        module_grads(attn_input, in_attn[2], grad_key_value[:, :, 1], out_key_value[1], weight),
        module_grads(attn_mixed, in_mixed, grad_attn_out, out_attn, weight),
        module_grads(mlp_input, in_mlp[0], grad_gate_up[:, :, 0], out_gate_up[0], weight),
        module_grads(mlp_input, in_mlp[1], grad_gate_up[:, :, 1], out_gate_up[1], weight),
        module_grads(hidden_acts, in_hidden, grad_mlp_out, out_mlp, weight),
    ]
    compressed = jnp.stack(blocks, axis=1).reshape(SEQS, -1)
    train_grads = compressed.astype(jnp.bfloat16)
    scores = lax.dot_general(train_grads, queries, (((1,), (1,)), ((), ())), preferred_element_type=jnp.float32)
    return train_grads, scores
```

```python
import functools
import jax
import jax.numpy as jnp
from jax import lax
from jax.experimental import pallas as pl
from jax.experimental.pallas import tpu as pltpu
from jax.sharding import PartitionSpec as P

BLOCK = 128
MODULES = 7
MESH = pl.DeviceIdType.MESH
NT = (((1,), (1,)), ((), ()))
TN = (((0,), (0,)), ((), ()))


def mm(a, b, dims=NT):
    return lax.dot_general(a, b, dims, preferred_element_type=jnp.float32)


def project_kernel(
    live_rows,
    table,
    attn_input,
    grad_query,
    grad_kv,
    attn_mixed,
    grad_attn,
    mlp_input,
    grad_gate_up,
    hidden,
    grad_mlp,
    in_attn,
    in_mixed,
    in_mlp,
    in_hidden,
    out_query,
    out_kv,
    out_attn,
    out_gate_up,
    out_mlp,
    out,
    w_attn,
    w_mlp,
    w_mixed,
    w_hidden,
    w_query,
    w_oattn,
    w_omlp,
    w_gu,
    w_kv,
    mixed_rows,
    rows,
    sem,
):
    i = pl.program_id(0)
    r = in_mixed.shape[0]

    @pl.when(i == 0)
    def _():
        for ref in (w_attn, w_mlp, w_mixed, w_hidden, w_query, w_oattn, w_omlp, w_gu, w_kv):
            ref[...] = jnp.zeros_like(ref)
        for m in range(3):
            w_attn[2 * r * m : 2 * r * m + r, :] = in_attn[m]
        for m in range(2):
            w_mlp[2 * r * m : 2 * r * m + r, :] = in_mlp[m]
            w_gu[2 * r * m + r : 2 * r * m + 2 * r, :] = out_gate_up[m]
            w_kv[m, :, r : 2 * r] = out_kv[m]
        w_mixed[:r, :] = in_mixed[...]
        w_hidden[:r, :] = in_hidden[...]
        w_query[r : 2 * r, :] = out_query[...]
        w_oattn[r : 2 * r, :] = out_attn[...]
        w_omlp[r : 2 * r, :] = out_mlp[...]

    @pl.when(table[3, i] > 0)
    def _():
        start = table[2, i]

        def put(m, value):
            rows[m, pl.ds(start, BLOCK), :] = value

        both = grad_gate_up[0].reshape(2 * BLOCK, grad_gate_up.shape[-1])
        rows_gu = mm(both, w_gu[...])
        mixed_rows[0] = rows_gu[:, : 2 * r]
        mixed_rows[1] = rows_gu[:, 2 * r :]
        first = mm(attn_input[0], w_attn[...])
        put(0, first[:, : 2 * r] + mm(grad_query[0], w_query[...]))
        put(1, first[:, 2 * r : 4 * r] + mm(grad_kv[0, 0], w_kv[0], TN))
        put(2, first[:, 4 * r :] + mm(grad_kv[0, 1], w_kv[1], TN))
        put(3, mm(attn_mixed[0], w_mixed[...]) + mm(grad_attn[0], w_oattn[...]))
        second = mm(mlp_input[0], w_mlp[...])
        put(4, second[:, : 2 * r] + mixed_rows[0, pl.ds(0, BLOCK, stride=2), :])
        put(5, second[:, 2 * r :] + mixed_rows[1, pl.ds(1, BLOCK, stride=2), :])
        put(6, mm(hidden[0], w_hidden[...]) + mm(grad_mlp[0], w_omlp[...]))

    @pl.when(i == pl.num_programs(0) - 1)
    def _():
        copy = pltpu.make_async_copy(rows.at[:, pl.ds(0, live_rows), :], out, sem)
        copy.start()
        copy.wait()


def project(arrays, lengths, live_rows):
    (
        attn_input, grad_query, grad_kv, attn_mixed, grad_attn, mlp_input, grad_gate_up, hidden, grad_mlp,
        in_attn, in_mixed, in_mlp, in_hidden, out_query, out_kv, out_attn, out_gate_up, out_mlp,
    ) = arrays
    seqs, maxlen = attn_input.shape[:2]
    r = in_mixed.shape[1]
    steps = maxlen // BLOCK + (live_rows - maxlen + (seqs - 1) * (BLOCK - 1)) // BLOCK
    counts = (lengths + BLOCK - 1) // BLOCK
    ends = jnp.cumsum(counts)
    starts = jnp.cumsum(lengths) - lengths
    ids = jnp.arange(steps, dtype=jnp.int32)
    at = jnp.minimum(ids, ends[-1] - 1)
    seq = jnp.sum((at[:, None] >= ends[None, :]).astype(jnp.int32), axis=1)
    pick = seq[:, None] == jnp.arange(seqs, dtype=jnp.int32)[None, :]
    first = jnp.sum(jnp.where(pick, (ends - counts)[None, :], 0), axis=1)
    begin = jnp.sum(jnp.where(pick, starts[None, :], 0), axis=1)
    block = at - first
    table = jnp.stack([seq, block, begin + block * BLOCK, (ids < ends[-1]).astype(jnp.int32)])

    grad_kv = jnp.transpose(grad_kv, (0, 2, 3, 1))
    tr = lambda x: jnp.swapaxes(x, -1, -2)
    factors = [
        tr(in_attn), tr(in_mixed), tr(in_mlp), tr(in_hidden), tr(out_query), out_kv, tr(out_attn),
        tr(out_gate_up), tr(out_mlp),
    ]
    data = [attn_input, grad_query, grad_kv, attn_mixed, grad_attn, mlp_input, grad_gate_up, hidden, grad_mlp]

    def spec(x):
        if x is grad_kv:
            return pl.BlockSpec((1,) + x.shape[1:3] + (BLOCK,), lambda i, t: (t[0, i], 0, 0, t[1, i]))
        rest = x.shape[2:]
        return pl.BlockSpec((1, BLOCK) + rest, lambda i, t: (t[0, i], t[1, i]) + (0,) * len(rest))

    def whole(x):
        return pl.BlockSpec(x.shape, lambda i, t: (0,) * x.ndim)

    bf = jnp.bfloat16
    width = attn_input.shape[2]
    ff = hidden.shape[2]
    return pl.pallas_call(
        functools.partial(project_kernel, live_rows),
        grid_spec=pltpu.PrefetchScalarGridSpec(
            num_scalar_prefetch=1,
            grid=(steps,),
            in_specs=[spec(x) for x in data] + [whole(x) for x in factors],
            out_specs=pl.BlockSpec(memory_space=pl.ANY),
            scratch_shapes=[
                pltpu.VMEM((6 * r, width), bf),
                pltpu.VMEM((4 * r, width), bf),
                pltpu.VMEM((2 * r, width), bf),
                pltpu.VMEM((2 * r, ff), bf),
                pltpu.VMEM((2 * r, width), bf),
                pltpu.VMEM((2 * r, width), bf),
                pltpu.VMEM((2 * r, width), bf),
                pltpu.VMEM((4 * r, ff), bf),
                pltpu.VMEM((2, grad_kv.shape[2], 2 * r), bf),
                pltpu.VMEM((2, 2 * BLOCK, 2 * r), jnp.float32),
                pltpu.VMEM((MODULES, live_rows + BLOCK, 2 * r), jnp.float32),
                pltpu.SemaphoreType.DMA,
            ],
        ),
        out_shape=jax.ShapeDtypeStruct((MODULES, live_rows, 2 * r), jnp.float32),
        compiler_params=pltpu.CompilerParams(vmem_limit_bytes=60 * 2**20),
    )(table, *data, *factors)


def reduce_kernel(n, bits, q_own, seqs, proj, weight, queries, grads_out, scores_out, *scratch):
    kept = scratch[0]
    bufs = scratch[1 : 1 + bits]
    send2 = scratch[1 + bits]
    bufs2 = scratch[2 + bits : 2 + 2 * bits]
    score = scratch[2 + 2 * bits]
    score_in = scratch[3 + 2 * bits]
    kept_sem, s1, r1, s2, r2, s3, r3 = scratch[4 + 2 * bits :]
    me = lax.axis_index("tensor")
    mine = [lax.rem(me // (1 << j), 2) for j in range(bits)]
    partner = [me + (1 - 2 * mine[j]) * (1 << j) for j in range(bits)]
    r = proj.shape[-1] // 2

    barrier = pltpu.get_barrier_semaphore()
    for j in range(bits):
        pl.semaphore_signal(barrier, inc=1, device_id={"tensor": partner[j]}, device_id_type=MESH)
    pl.semaphore_wait(barrier, bits)

    def part(ref, lead, j, which):
        return ref.at[lead + (slice(None),) * (bits - 1 - j) + (which,)]

    def send(ref, lead, into, into_lead, j, ss, rs):
        return pltpu.make_async_remote_copy(
            src_ref=part(ref, lead, j, 1 - mine[j]),
            dst_ref=into.at[into_lead] if into_lead else into,
            send_sem=ss,
            recv_sem=rs,
            device_id={"tensor": partner[j]},
            device_id_type=MESH,
        )

    def copy1(m, j):
        source = proj if j == 0 else bufs[j - 1]
        return send(source, (m,), bufs[j], (m,), j, s1.at[m, j], r1.at[m, j])

    def keep(m):
        return pltpu.make_async_copy(part(proj, (m,), 0, mine[0]), kept.at[m], kept_sem.at[m])

    for m in range(MODULES):
        copy1(m, 0).start()
        keep(m).start()

    def take(m, j):
        copy1(m, j).wait()
        if j == 0:
            keep(m).wait()
            bufs[0][m] = bufs[0][m] + kept[m]
        else:
            bufs[j][m] = bufs[j][m] + part(bufs[j - 1], (m,), j, mine[j])[...]
        if j + 1 < bits:
            copy1(m, j + 1).start()

    rows_own = send2.shape[-2]
    w = weight[...]
    lane = lax.broadcasted_iota(jnp.int32, (w.shape[0], 2 * r), 1)

    def outer(m):
        x = bufs[bits - 1][m]
        double = jnp.where(lane < r, pltpu.roll(x, r, 1), x)
        right = jnp.concatenate([double] * (seqs // 2), axis=1) * w
        value = lax.dot_general(
            x, right, TN, preferred_element_type=jnp.float32, precision=lax.Precision.HIGHEST
        )[:r]
        low = m * r
        while low < (m + 1) * r:
            owner, inside = divmod(low, rows_own)
            count = min(rows_own - inside, (m + 1) * r - low)
            index = tuple((owner >> b) & 1 for b in reversed(range(bits)))
            begin = low - m * r
            send2[index + (slice(inside, inside + count), slice(None))] = value[begin : begin + count]
            low += count

    for m in range(MODULES):
        take(m, 0)
    for d in range(MODULES + bits - 2):
        for j in range(bits - 1, 0, -1):
            m = d - (j - 1)
            if 0 <= m < MODULES:
                take(m, j)
                if j == bits - 1:
                    outer(m)

    for j in range(bits):
        source = send2 if j == 0 else bufs2[j - 1]
        copy = send(source, (), bufs2[j], (), j, s2.at[j], r2.at[j])
        copy.start()
        copy.wait()
        bufs2[j][...] = bufs2[j][...] + part(source, (), j, mine[j])[...]

    grads = bufs2[bits - 1][...].astype(jnp.bfloat16)
    exact = grads.astype(jnp.float32)
    features = queries.shape[1]
    tiles = pl.cdiv(features, 2 * r)
    lane_row = lax.broadcasted_iota(jnp.int32, (rows_own, tiles * 2 * r), 1) // r
    own_row = lax.broadcasted_iota(jnp.int32, (rows_own, tiles * 2 * r), 0)
    half = lax.broadcasted_iota(jnp.int32, (rows_own, 2 * r), 1) < r
    flat = []
    for s in range(seqs):
        pair = exact[:, (s // 2) * 2 * r : (s // 2 + 1) * 2 * r]
        other = pltpu.roll(pair, r, 1)
        double = jnp.where(half, pair, other) if s % 2 == 0 else jnp.where(half, other, pair)
        spread = jnp.concatenate([double] * tiles, axis=1)
        flat.append(jnp.sum(jnp.where(lane_row == own_row, spread, 0.0), axis=0, keepdims=True))
    flat = jnp.concatenate(flat + [jnp.zeros_like(flat[0])] * (8 - seqs), axis=0)
    flat = flat[:, :features].astype(jnp.bfloat16)
    grads_out[...] = flat[:seqs]
    score[0] = mm(flat, queries[...])

    for j in range(bits):
        copy = pltpu.make_async_remote_copy(
            src_ref=score.at[j],
            dst_ref=score_in.at[j],
            send_sem=s3.at[j],
            recv_sem=r3.at[j],
            device_id={"tensor": partner[j]},
            device_id_type=MESH,
        )
        copy.start()
        copy.wait()
        score[j + 1] = score[j] + score_in[j]
    total = score[bits]
    result = jnp.zeros((seqs, q_own), jnp.float32)
    for d in range(n):
        result = jnp.where(me == d, total[:seqs, d * q_own : (d + 1) * q_own], result)
    scores_out[...] = result


def reduce_and_score(n, proj, weight, queries, seqs):
    bits = n.bit_length() - 1
    modules, live, lanes = proj.shape
    r = lanes // 2
    rows = live // n
    rows_own = modules * r // n
    q_own = queries.shape[0] // n
    proj = proj.reshape((modules,) + (2,) * bits + (rows, lanes))
    f32 = jnp.float32
    dma = pltpu.SemaphoreType.DMA
    vmem = pl.BlockSpec(memory_space=pltpu.VMEM)
    return pl.pallas_call(
        functools.partial(reduce_kernel, n, bits, q_own, seqs),
        in_specs=[pl.BlockSpec(memory_space=pl.ANY), vmem, vmem],
        out_specs=[vmem, vmem],
        out_shape=[
            jax.ShapeDtypeStruct((seqs, rows_own * r), jnp.bfloat16),
            jax.ShapeDtypeStruct((seqs, q_own), f32),
        ],
        scratch_shapes=[pltpu.VMEM((modules,) + (2,) * (bits - 1) + (rows, lanes), f32)]
        + [pltpu.VMEM((modules,) + (2,) * (bits - 1 - j) + (rows, lanes), f32) for j in range(bits)]
        + [pltpu.VMEM((2,) * bits + (rows_own, seqs * r), f32)]
        + [pltpu.VMEM((2,) * (bits - 1 - j) + (rows_own, seqs * r), f32) for j in range(bits)]
        + [
            pltpu.VMEM((bits + 1, 8, queries.shape[0]), f32),
            pltpu.VMEM((bits, 8, queries.shape[0]), f32),
            dma((modules,)),
            dma((modules, bits)),
            dma((modules, bits)),
            dma((bits,)),
            dma((bits,)),
            dma((bits,)),
            dma((bits,)),
        ],
        compiler_params=pltpu.CompilerParams(
            collective_id=0, has_side_effects=True, vmem_limit_bytes=60 * 2**20
        ),
    )(proj, weight, queries)


def body(n, *arrays):
    queries, lengths = arrays[18], arrays[19]
    seqs, maxlen = arrays[0].shape[:2]
    r = arrays[10].shape[1]
    live = seqs * maxlen // 2
    proj = project(arrays[:18], lengths, live)
    rows = live // n
    ids = lax.axis_index("tensor") * rows + jnp.arange(rows, dtype=jnp.int32)
    ends = jnp.cumsum(lengths)
    inside = (ids[:, None] >= (ends - lengths)[None, :]) & (ids[:, None] < ends[None, :])
    weight = inside.astype(jnp.float32) / lengths.astype(jnp.float32)[None, :]
    weight = jnp.repeat(weight, r, axis=1)
    return reduce_and_score(n, proj, weight, queries, seqs)


def solution(mesh):
    features = P("dom", None, "tensor")
    pair = P("dom", None, None, "tensor")
    one, many = P("tensor", None), P(None, "tensor", None)
    return jax.shard_map(
        functools.partial(body, mesh.shape["tensor"]),
        mesh=mesh,
        in_specs=(
            features, features, pair, features, features, features, pair, features, features,
            many, one, many, one, one, many, one, many, one, P(None, "tensor"), P("dom"),
        ),
        out_specs=(P("dom", "tensor"), P("dom", "tensor")),
        check_vma=False,
    )
```

```python
import functools
import jax
import jax.numpy as jnp
from jax import lax
from jax.experimental import pallas as pl
from jax.experimental.pallas import tpu as pltpu
from jax.sharding import PartitionSpec as P

BLOCK = 128
MODULES = 7
MESH = pl.DeviceIdType.MESH
NT = (((1,), (1,)), ((), ()))
TN = (((0,), (0,)), ((), ()))


def mm(a, b, dims=NT):
    return lax.dot_general(a, b, dims, preferred_element_type=jnp.float32)


def project_kernel(
    live_rows,
    table,
    attn_input,
    grad_query,
    grad_kv,
    attn_mixed,
    grad_attn,
    mlp_input,
    grad_gate_up,
    hidden,
    grad_mlp,
    in_attn,
    in_mixed,
    in_mlp,
    in_hidden,
    out_query,
    out_kv,
    out_attn,
    out_gate_up,
    out_mlp,
    out,
    w_attn,
    w_mlp,
    w_mixed,
    w_hidden,
    w_query,
    w_oattn,
    w_omlp,
    w_gu,
    w_kv,
    mixed_rows,
    rows,
    sem,
):
    i = pl.program_id(0)
    r = in_mixed.shape[0]

    @pl.when(i == 0)
    def _():
        for ref in (w_attn, w_mlp, w_mixed, w_hidden, w_query, w_oattn, w_omlp, w_gu, w_kv):
            ref[...] = jnp.zeros_like(ref)
        for m in range(3):
            w_attn[2 * r * m : 2 * r * m + r, :] = in_attn[m]
        for m in range(2):
            w_mlp[2 * r * m : 2 * r * m + r, :] = in_mlp[m]
            w_gu[2 * r * m + r : 2 * r * m + 2 * r, :] = out_gate_up[m]
            w_kv[m, :, r : 2 * r] = out_kv[m]
        w_mixed[:r, :] = in_mixed[...]
        w_hidden[:r, :] = in_hidden[...]
        w_query[r : 2 * r, :] = out_query[...]
        w_oattn[r : 2 * r, :] = out_attn[...]
        w_omlp[r : 2 * r, :] = out_mlp[...]

    @pl.when(table[3, i] > 0)
    def _():
        start = table[2, i]

        def put(m, value):
            rows[m, pl.ds(start, BLOCK), :] = value

        both = grad_gate_up[0].reshape(2 * BLOCK, grad_gate_up.shape[-1])
        rows_gu = mm(both, w_gu[...])
        mixed_rows[0] = rows_gu[:, : 2 * r]
        mixed_rows[1] = rows_gu[:, 2 * r :]
        first = mm(attn_input[0], w_attn[...])
        put(0, first[:, : 2 * r] + mm(grad_query[0], w_query[...]))
        put(1, first[:, 2 * r : 4 * r] + mm(grad_kv[0, 0], w_kv[0], TN))
        put(2, first[:, 4 * r :] + mm(grad_kv[0, 1], w_kv[1], TN))
        put(3, mm(attn_mixed[0], w_mixed[...]) + mm(grad_attn[0], w_oattn[...]))
        second = mm(mlp_input[0], w_mlp[...])
        put(4, second[:, : 2 * r] + mixed_rows[0, pl.ds(0, BLOCK, stride=2), :])
        put(5, second[:, 2 * r :] + mixed_rows[1, pl.ds(1, BLOCK, stride=2), :])
        put(6, mm(hidden[0], w_hidden[...]) + mm(grad_mlp[0], w_omlp[...]))

    @pl.when(i == pl.num_programs(0) - 1)
    def _():
        copy = pltpu.make_async_copy(rows.at[:, pl.ds(0, live_rows), :], out, sem)
        copy.start()
        copy.wait()


def project(arrays, lengths, live_rows):
    (
        attn_input, grad_query, grad_kv, attn_mixed, grad_attn, mlp_input, grad_gate_up, hidden, grad_mlp,
        in_attn, in_mixed, in_mlp, in_hidden, out_query, out_kv, out_attn, out_gate_up, out_mlp,
    ) = arrays
    seqs, maxlen = attn_input.shape[:2]
    r = in_mixed.shape[1]
    steps = maxlen // BLOCK + (live_rows - maxlen + (seqs - 1) * (BLOCK - 1)) // BLOCK
    ids = jnp.arange(steps, dtype=jnp.int32)
    sizes = [lengths[s] for s in range(seqs)]
    counts = [(size + BLOCK - 1) // BLOCK for size in sizes]
    total = sum(counts)
    at = jnp.minimum(ids, total - 1)
    seq, block, start = jnp.zeros_like(ids), at, jnp.zeros_like(ids)
    end = 0
    for size, count in zip(sizes[:-1], counts[:-1]):
        end = end + count
        past = at >= end
        seq = seq + past.astype(jnp.int32)
        block = block - jnp.where(past, count, 0)
        start = start + jnp.where(past, size, 0)
    table = jnp.stack([seq, block, start + block * BLOCK, (ids < total).astype(jnp.int32)])

    grad_kv = jnp.transpose(grad_kv, (0, 2, 3, 1))
    tr = lambda x: jnp.swapaxes(x, -1, -2)
    factors = [
        tr(in_attn), tr(in_mixed), tr(in_mlp), tr(in_hidden), tr(out_query), out_kv, tr(out_attn),
        tr(out_gate_up), tr(out_mlp),
    ]
    data = [attn_input, grad_query, grad_kv, attn_mixed, grad_attn, mlp_input, grad_gate_up, hidden, grad_mlp]

    def spec(x):
        if x is grad_kv:
            return pl.BlockSpec((1,) + x.shape[1:3] + (BLOCK,), lambda i, t: (t[0, i], 0, 0, t[1, i]))
        rest = x.shape[2:]
        return pl.BlockSpec((1, BLOCK) + rest, lambda i, t: (t[0, i], t[1, i]) + (0,) * len(rest))

    def whole(x):
        return pl.BlockSpec(x.shape, lambda i, t: (0,) * x.ndim)

    bf = jnp.bfloat16
    width = attn_input.shape[2]
    ff = hidden.shape[2]
    return pl.pallas_call(
        functools.partial(project_kernel, live_rows),
        grid_spec=pltpu.PrefetchScalarGridSpec(
            num_scalar_prefetch=1,
            grid=(steps,),
            in_specs=[spec(x) for x in data] + [whole(x) for x in factors],
            out_specs=pl.BlockSpec(memory_space=pl.ANY),
            scratch_shapes=[
                pltpu.VMEM((6 * r, width), bf),
                pltpu.VMEM((4 * r, width), bf),
                pltpu.VMEM((2 * r, width), bf),
                pltpu.VMEM((2 * r, ff), bf),
                pltpu.VMEM((2 * r, width), bf),
                pltpu.VMEM((2 * r, width), bf),
                pltpu.VMEM((2 * r, width), bf),
                pltpu.VMEM((4 * r, ff), bf),
                pltpu.VMEM((2, grad_kv.shape[2], 2 * r), bf),
                pltpu.VMEM((2, 2 * BLOCK, 2 * r), jnp.float32),
                pltpu.VMEM((MODULES, live_rows + BLOCK, 2 * r), jnp.float32),
                pltpu.SemaphoreType.DMA,
            ],
        ),
        out_shape=jax.ShapeDtypeStruct((MODULES, live_rows, 2 * r), jnp.float32),
        compiler_params=pltpu.CompilerParams(vmem_limit_bytes=60 * 2**20),
    )(table, *data, *factors)


def reduce_kernel(n, bits, q_own, seqs, lengths, proj, queries, grads_out, scores_out, *scratch):
    kept = scratch[0]
    bufs = scratch[1 : 1 + bits]
    send2 = scratch[1 + bits]
    bufs2 = scratch[2 + bits : 2 + 2 * bits]
    score = scratch[2 + 2 * bits]
    score_in = scratch[3 + 2 * bits]
    kept_sem, s1, r1, s2, r2, s3, r3 = scratch[4 + 2 * bits :]
    me = lax.axis_index("tensor")
    mine = [lax.rem(me // (1 << j), 2) for j in range(bits)]
    r = proj.shape[-1] // 2

    def peer(mask):
        return me + sum((1 - 2 * mine[b]) * (1 << b) for b in range(bits) if mask >> b & 1)

    groups = [[1 << b, 2 << b, 3 << b] if b + 1 < bits else [1 << b] for b in range(0, bits, 2)]
    partners = [mask for group in groups for mask in group]
    straight = list(range(bits))
    swapped = [0, 2, 1] + straight[3:] if bits > 3 else straight
    orders = [swapped if m in (1, 4) else straight for m in range(MODULES)]
    halves = [straight, swapped]

    barrier = pltpu.get_barrier_semaphore()
    for mask in partners:
        pl.semaphore_signal(barrier, inc=1, device_id={"tensor": peer(mask)}, device_id_type=MESH)
    pl.semaphore_wait(barrier, len(partners))

    def part(ref, lead, order, j, other):
        bit = order[j]
        ahead = sum(b > bit for b in order[j:])
        which = 1 - mine[bit] if other else mine[bit]
        return ref.at[lead + (slice(None),) * ahead + (which,)]

    def send(ref, lead, into, order, j, ss, rs):
        return pltpu.make_async_remote_copy(
            src_ref=part(ref, lead, order, j, True),
            dst_ref=into.at[lead],
            send_sem=ss,
            recv_sem=rs,
            device_id={"tensor": peer(1 << order[j])},
            device_id_type=MESH,
        )

    def copy1(m, j):
        source = proj if j == 0 else bufs[j - 1]
        return send(source, (m,), bufs[j], orders[m], j, s1.at[m, j], r1.at[m, j])

    def keep(m):
        return pltpu.make_async_copy(part(proj, (m,), orders[m], 0, False), kept.at[m], kept_sem.at[m])

    for m in range(MODULES):
        copy1(m, 0).start()
        keep(m).start()

    def take(m, j):
        copy1(m, j).wait()
        if j == 0:
            keep(m).wait()
            bufs[0][m] = bufs[0][m] + kept[m]
        else:
            bufs[j][m] = bufs[j][m] + part(bufs[j - 1], (m,), orders[m], j, False)[...]
        if j + 1 < bits:
            copy1(m, j + 1).start()

    rows_own = send2.shape[-2]
    rows = proj.shape[-2]
    lane = lax.broadcasted_iota(jnp.int32, (rows, 2 * r), 1)
    ids = lax.broadcasted_iota(jnp.int32, (rows, 2 * r), 0) + me * rows
    sizes = [lengths[s] for s in range(seqs)]
    weights = []
    begin = 0
    for size in sizes:
        inside = (ids >= begin) & (ids < begin + size)
        size = jnp.broadcast_to(size, ids.shape).astype(jnp.float32)
        weights.append(jnp.where(inside, 1.0 / size, 0.0))
        begin = begin + sizes[len(weights) - 1]
    w = jnp.concatenate(
        [jnp.where(lane < r, weights[s], weights[s + 1]) for s in range(0, seqs, 2)], axis=1
    )

    half2 = send2.shape[-1]

    def outer(m):
        x = bufs[bits - 1][m]
        double = jnp.where(lane < r, pltpu.roll(x, r, 1), x)
        right = jnp.concatenate([double] * (seqs // 2), axis=1) * w
        value = lax.dot_general(
            x, right, TN, preferred_element_type=jnp.float32, precision=lax.Precision.HIGHEST
        )[:r]
        low = m * r
        while low < (m + 1) * r:
            owner, inside = divmod(low, rows_own)
            count = min(rows_own - inside, (m + 1) * r - low)
            index = tuple((owner >> b) & 1 for b in reversed(range(bits)))
            begin = low - m * r
            for h in range(2):
                send2[(h,) + index + (slice(inside, inside + count), slice(None))] = value[
                    begin : begin + count, h * half2 : (h + 1) * half2
                ]
            low += count

    for m in range(MODULES):
        take(m, 0)
    for d in range(MODULES + bits - 2):
        for j in range(bits - 1, 0, -1):
            m = d - (j - 1)
            if 0 <= m < MODULES:
                take(m, j)
                if j == bits - 1:
                    outer(m)

    def copy2(h, j):
        source = send2 if j == 0 else bufs2[j - 1]
        return send(source, (h,), bufs2[j], halves[h], j, s2.at[h, j], r2.at[h, j])

    for h in range(2):
        copy2(h, 0).start()
    for j in range(bits):
        for h in range(2):
            copy2(h, j).wait()
            source = send2 if j == 0 else bufs2[j - 1]
            bufs2[j][h] = bufs2[j][h] + part(source, (h,), halves[h], j, False)[...]
            if j + 1 < bits:
                copy2(h, j + 1).start()

    grads = jnp.concatenate([bufs2[bits - 1][h] for h in range(2)], axis=1).astype(jnp.bfloat16)
    exact = grads.astype(jnp.float32)
    features = queries.shape[1]
    tiles = pl.cdiv(features, 2 * r)
    lane_row = lax.broadcasted_iota(jnp.int32, (rows_own, tiles * 2 * r), 1) // r
    own_row = lax.broadcasted_iota(jnp.int32, (rows_own, tiles * 2 * r), 0)
    half = lax.broadcasted_iota(jnp.int32, (rows_own, 2 * r), 1) < r
    flat = []
    for s in range(seqs):
        pair = exact[:, (s // 2) * 2 * r : (s // 2 + 1) * 2 * r]
        other = pltpu.roll(pair, r, 1)
        double = jnp.where(half, pair, other) if s % 2 == 0 else jnp.where(half, other, pair)
        spread = jnp.concatenate([double] * tiles, axis=1)
        flat.append(jnp.sum(jnp.where(lane_row == own_row, spread, 0.0), axis=0, keepdims=True))
    flat = jnp.concatenate(flat + [jnp.zeros_like(flat[0])] * (8 - seqs), axis=0)
    flat = flat[:, :features].astype(jnp.bfloat16)
    grads_out[...] = flat[:seqs]
    score[0] = mm(flat, queries[...])

    at = 0
    for g, group in enumerate(groups):
        copies = [
            pltpu.make_async_remote_copy(
                src_ref=score.at[g],
                dst_ref=score_in.at[at + k],
                send_sem=s3.at[at + k],
                recv_sem=r3.at[at + k],
                device_id={"tensor": peer(mask)},
                device_id_type=MESH,
            )
            for k, mask in enumerate(group)
        ]
        for copy in copies:
            copy.start()
        total = score[g]
        for k, copy in enumerate(copies):
            copy.wait()
            total = total + score_in[at + k]
        score[g + 1] = total
        at += len(group)
    total = score[len(groups)]
    result = jnp.zeros((seqs, q_own), jnp.float32)
    for d in range(n):
        result = jnp.where(me == d, total[:seqs, d * q_own : (d + 1) * q_own], result)
    scores_out[...] = result


def reduce_and_score(n, proj, lengths, queries, seqs):
    bits = n.bit_length() - 1
    modules, live, lanes = proj.shape
    r = lanes // 2
    rows = live // n
    rows_own = modules * r // n
    q_own = queries.shape[0] // n
    proj = proj.reshape((modules,) + (2,) * bits + (rows, lanes))
    f32 = jnp.float32
    dma = pltpu.SemaphoreType.DMA
    vmem = pl.BlockSpec(memory_space=pltpu.VMEM)
    return pl.pallas_call(
        functools.partial(reduce_kernel, n, bits, q_own, seqs),
        in_specs=[pl.BlockSpec(memory_space=pltpu.SMEM), pl.BlockSpec(memory_space=pl.ANY), vmem],
        out_specs=[vmem, vmem],
        out_shape=[
            jax.ShapeDtypeStruct((seqs, rows_own * r), jnp.bfloat16),
            jax.ShapeDtypeStruct((seqs, q_own), f32),
        ],
        scratch_shapes=[pltpu.VMEM((modules,) + (2,) * (bits - 1) + (rows, lanes), f32)]
        + [pltpu.VMEM((modules,) + (2,) * (bits - 1 - j) + (rows, lanes), f32) for j in range(bits)]
        + [pltpu.VMEM((2,) * (bits + 1) + (rows_own, seqs * r // 2), f32)]
        + [pltpu.VMEM((2,) * (bits - j) + (rows_own, seqs * r // 2), f32) for j in range(bits)]
        + [
            pltpu.VMEM((bits + 1, 8, queries.shape[0]), f32),
            pltpu.VMEM((3 * bits, 8, queries.shape[0]), f32),
            dma((modules,)),
            dma((modules, bits)),
            dma((modules, bits)),
            dma((2, bits)),
            dma((2, bits)),
            dma((3 * bits,)),
            dma((3 * bits,)),
        ],
        compiler_params=pltpu.CompilerParams(
            collective_id=0, has_side_effects=True, vmem_limit_bytes=60 * 2**20
        ),
    )(lengths, proj, queries)


def body(n, *arrays):
    queries, lengths = arrays[18], arrays[19]
    seqs, maxlen = arrays[0].shape[:2]
    live = seqs * maxlen // 2
    proj = project(arrays[:18], lengths, live)
    return reduce_and_score(n, proj, lengths, queries, seqs)


def solution(mesh):
    features = P("dom", None, "tensor")
    pair = P("dom", None, None, "tensor")
    one, many = P("tensor", None), P(None, "tensor", None)
    return jax.shard_map(
        functools.partial(body, mesh.shape["tensor"]),
        mesh=mesh,
        in_specs=(
            features, features, pair, features, features, features, pair, features, features,
            many, one, many, one, one, many, one, many, one, P(None, "tensor"), P("dom"),
        ),
        out_specs=(P("dom", "tensor"), P("dom", "tensor")),
        check_vma=False,
    )
```
